32 devices in a mesh: rep: 16 (over z, y, core), shard: 2 (over x).
Axes of the slice: x: 2, y: 2, z: 4, core: 2. Of those that a mesh axis runs over, the one named last changes fastest.
Arguments:
- grad_xproj: bfloat16 [64, 2, 3072, 128], P(('rep', 'shard')), may hold values from -32 to 32
- grad_chan: bfloat16 [64, 2, 118, 3072], P(('rep', 'shard')), may hold values from -32 to 32
- grad_embed: bfloat16 [64, 1024, 1536], P(('rep', 'shard')), may hold values from -32 to 32
- weight_xproj: float32 [2, 3072, 128], P(None, 'shard'), may hold values from -0.3125 to 0.3125
- weight_chan: float32 [2, 118, 3072], P(None, None, 'shard'), may hold values from -0.3125 to 0.3125
- weight_embed: float32 [1024, 1536], P('shard'), may hold values from -0.3125 to 0.3125
- moment_xproj: float32 [2, 3072, 128], P(None, 'shard'), may hold values from -0.015625 to 0.015625
- moment_chan: float32 [2, 118, 3072], P(None, None, 'shard'), may hold values from -0.015625 to 0.015625
- moment_embed: float32 [1024, 1536], P('shard'), may hold values from -0.015625 to 0.015625
- second_xproj: float32 [2, 3072, 128], P(None, 'shard'), may hold values from 1e-08 to 1e-05
- second_chan: float32 [2, 118, 3072], P(None, None, 'shard'), may hold values from 1e-08 to 1e-05
- second_embed: float32 [1024, 1536], P('shard'), may hold values from 1e-08 to 1e-05
Outputs:
- new_weight_xproj: float32 [2, 3072, 128], P(None, 'shard')
- new_weight_chan: float32 [2, 118, 3072], P(None, None, 'shard')
- new_weight_embed: float32 [1024, 1536], P('shard')
- new_moment_xproj: float32 [2, 3072, 128], P(None, 'shard')
- new_moment_chan: float32 [2, 118, 3072], P(None, None, 'shard')
- new_moment_embed: float32 [1024, 1536], P('shard')
- new_second_xproj: float32 [2, 3072, 128], P(None, 'shard')
- new_second_chan: float32 [2, 118, 3072], P(None, None, 'shard')
- new_second_embed: float32 [1024, 1536], P('shard')
- full_xproj: bfloat16 [2, 3072, 128], replicated
- full_chan: bfloat16 [2, 118, 3072], replicated
- full_embed: bfloat16 [1024, 1536], replicated
- pre_norm: float32 [1], replicated
The draws below stay inside these ranges and needn't reach their ends.
All inputs are finite; a program needn't handle non-finite values.
Results may differ from the reference program's by a relative error of at most 0.00085.
Values may be sent and summed in bfloat16 or wider, within the bound.
A program may use at most 448 MiB of HBM per device.

```python
import math
import jax
import jax.numpy as jnp
from jax import lax

D = 1536
INNER = 3072
LAYERS = 2
MICRO = 2
EMB_ROWS = 1024
XW = 128
CH = 118
GRADS = 64


def along_dim(vector, dim, rank):
    dims_list = [1] * rank
    dims_list[dim] = vector.shape[0]
    return jnp.reshape(vector, tuple(dims_list))


def gradient_draw(key, full_shape, src_dim, dst_dim):
    rank = len(full_shape)
    devices = GRADS // MICRO
    values = jnp.clip(jax.random.normal(key, full_shape, jnp.float32), -4.5, 4.5)
    ramp_power = 0.5
    pairing = jax.random.permutation(jax.random.fold_in(key, 11), devices).astype(jnp.int32)
    owning = jnp.arange(full_shape[src_dim], dtype=jnp.int32) // MICRO
    target = jnp.take(pairing, owning)
    length = full_shape[dst_dim]
    position = jnp.arange(length, dtype=jnp.int32)
    blocks_at = position // (length // devices)
    spike_scale = jnp.where(along_dim(target, src_dim, rank) == along_dim(blocks_at, dst_dim, rank), 4.0, 1.0)
    ramp_scale = jnp.exp(ramp_power * math.log(3.0) * position.astype(jnp.float32) / length)
    return values * spike_scale * along_dim(ramp_scale, dst_dim, rank)


def draw_grad_xproj(key, part):
    return gradient_draw(jax.random.fold_in(key, 101), (GRADS, LAYERS, INNER, XW), 0, 2).astype(jnp.bfloat16)


def draw_grad_chan(key, part):
    return gradient_draw(jax.random.fold_in(key, 202), (GRADS, LAYERS, CH, INNER), 0, 3).astype(jnp.bfloat16)


def draw_grad_embed(key, part):
    return gradient_draw(jax.random.fold_in(key, 303), (GRADS, EMB_ROWS, D), 0, 1).astype(jnp.bfloat16)


def steps_of(stream_key, extent, cuts, low, top_value):
    factor_of, own = 1.0, jax.random.fold_in(stream_key, 6)
    for dim, parts in cuts:
        heights = jnp.exp(jax.random.uniform(jax.random.fold_in(own, dim), (parts,), jnp.float32, low / len(cuts), top_value / len(cuts)))
        factor_of = factor_of * jnp.repeat(heights, extent[dim] // parts).reshape([-1 if axis == dim else 1 for axis in range(len(extent))])
    return factor_of


def scatter_about(own_key, extent, deviation, reach, split=(), held_as=jnp.bfloat16):
    result = deviation * jax.random.normal(own_key, extent, jnp.float32)
    if split:
        result = result * steps_of(own_key, extent, split, -0.22, 0.18)
    return jnp.clip(result, -reach, reach).astype(held_as)


def setup_inputs(seed: int = 0) -> dict:
    keys = jax.random.split(jax.random.key(seed), 13)
    return {
        "grad_xproj": draw_grad_xproj(jax.random.fold_in(keys[12], 71), 0),
        "grad_chan": draw_grad_chan(jax.random.fold_in(keys[12], 71), 0),
        "grad_embed": draw_grad_embed(jax.random.fold_in(keys[12], 71), 0),
        "weight_xproj": scatter_about(keys[3], (LAYERS, INNER, XW), 0.02, 0.3125, ((1, 2),), jnp.float32),
        "weight_chan": scatter_about(keys[4], (LAYERS, CH, INNER), 0.02, 0.3125, ((2, 2),), jnp.float32),
        "weight_embed": scatter_about(keys[5], (EMB_ROWS, D), 0.02, 0.3125, ((0, 2),), jnp.float32),
        "moment_xproj": scatter_about(keys[6], (LAYERS, INNER, XW), 0.001, 0.015625, ((1, 2),), jnp.float32),
        "moment_chan": scatter_about(keys[7], (LAYERS, CH, INNER), 0.001, 0.015625, ((2, 2),), jnp.float32),
        "moment_embed": scatter_about(keys[8], (EMB_ROWS, D), 0.001, 0.015625, ((0, 2),), jnp.float32),
        "second_xproj": jnp.clip(jnp.exp(math.log(9.999999747378752e-06) - 6.9077553 * jax.random.uniform(keys[9], (LAYERS, INNER, XW), jnp.float32) ** steps_of(keys[9], (LAYERS, INNER, XW), ((1, 2),), -0.2, 0.2)), 9.99999993922529e-09, 9.999999747378752e-06),
        "second_chan": jnp.clip(jnp.exp(math.log(9.999999747378752e-06) - 6.9077553 * jax.random.uniform(keys[10], (LAYERS, CH, INNER), jnp.float32) ** steps_of(keys[10], (LAYERS, CH, INNER), ((2, 2),), -0.2, 0.2)), 9.99999993922529e-09, 9.999999747378752e-06),
        "second_embed": jnp.clip(jnp.exp(math.log(9.999999747378752e-06) - 6.9077553 * jax.random.uniform(keys[11], (EMB_ROWS, D), jnp.float32) ** steps_of(keys[11], (EMB_ROWS, D), ((0, 2),), -0.2, 0.2)), 9.99999993922529e-09, 9.999999747378752e-06),
    }


beta_one = 0.9
beta_two = 0.999
learn_rate = 0.003
decay_rate = 0.1
epsilon = 1e-08
correct_one = 0.9999734386011124
correct_two = 0.09520785288629094

def mean_grad(gradients):
    return lax.optimization_barrier(jnp.sum(gradients, axis=0, dtype=jnp.float32)) / gradients.shape[0]

def adamw_update(weight, moment, second, gradient, clip_factor):
    clipped = clip_factor * gradient
    new_moment = beta_one * moment + (1.0 - beta_one) * clipped
    new_second = beta_two * second + (1.0 - beta_two) * clipped * clipped
    step_size = new_moment / correct_one / (jnp.sqrt(new_second / correct_two) + epsilon)
    new_weight = weight - learn_rate * (step_size + decay_rate * weight)
    return (new_weight, new_moment, new_second)

def reference(grad_xproj, grad_chan, grad_embed, weight_xproj, weight_chan, weight_embed, moment_xproj, moment_chan, moment_embed, second_xproj, second_chan, second_embed):
    mean_x = mean_grad(grad_xproj)
    mean_c = mean_grad(grad_chan)
    mean_e = mean_grad(grad_embed)
    squares = jnp.sum(mean_x * mean_x) + jnp.sum(mean_c * mean_c) + jnp.sum(mean_e * mean_e)
    norm_value = jnp.sqrt(squares)
    clip_factor = jnp.minimum(1.0, 1.0 / (norm_value + 1e-06))
    wx, mx, vx = adamw_update(weight_xproj, moment_xproj, second_xproj, mean_x, clip_factor)
    wc, mc, vc = adamw_update(weight_chan, moment_chan, second_chan, mean_c, clip_factor)
    we, me, ve = adamw_update(weight_embed, moment_embed, second_embed, mean_e, clip_factor)
    return (wx, wc, we, mx, mc, me, vx, vc, ve, wx.astype(jnp.bfloat16), wc.astype(jnp.bfloat16), we.astype(jnp.bfloat16), jnp.reshape(norm_value, (1,)))
```

```python
import functools

import jax
import jax.numpy as jnp
from jax import lax
from jax.experimental import pallas as pl
from jax.experimental.pallas import tpu as pltpu
from jax.sharding import PartitionSpec as P

beta_one = 0.9
beta_two = 0.999
learn_rate = 0.003
decay_rate = 0.1
epsilon = 1e-08
correct_one = 0.9999734386011124
correct_two = 0.09520785288629094

F32 = jnp.float32
BF16 = jnp.bfloat16
MESH = pl.DeviceIdType.MESH
VMEM = pl.BlockSpec(memory_space=pltpu.VMEM)
HBM = pl.BlockSpec(memory_space=pl.ANY)
PIECES = ((32, 1536), (192, 128), (64, 384))
TAIL = 54
LIMIT = 52 * 1024 * 1024


def adamw_update(weight, moment, second, gradient, clip_factor):
    clipped = clip_factor * gradient
    new_moment = beta_one * moment + (1.0 - beta_one) * clipped
    new_second = beta_two * second + (1.0 - beta_two) * clipped * clipped
    root = jnp.sqrt(new_second * (1.0 / correct_two)) + epsilon
    step_size = new_moment * (1.0 / correct_one) / root
    new_weight = weight - learn_rate * (step_size + decay_rate * weight)
    return (new_weight, new_moment, new_second)


def sum_embed(g_ref, o_ref):
    o_ref[...] = (g_ref[0].astype(F32) + g_ref[1].astype(F32)).astype(BF16)


def sum_xproj(g_ref, o_ref):
    o_ref[0, 0] = (g_ref[0, 0].astype(F32) + g_ref[1, 0].astype(F32)).astype(BF16)


def sum_chan(g_ref, o_ref):
    for c in range(2):
        rows = 64 if c == 0 else TAIL
        for z in range(4):
            at = (0, slice(c * 64, c * 64 + rows), slice(z * 384, z * 384 + 384))
            total = g_ref[(0, *at)].astype(F32) + g_ref[(1, *at)].astype(F32)
            if rows < 64:
                o_ref[0, c, 0, z] = jnp.zeros((64, 384), BF16)
            o_ref[0, c, 0, z, 0:rows] = total.astype(BF16)


def local_sums(grad_e, grad_x, grad_c):
    e = pl.pallas_call(
        sum_embed,
        grid=(8,),
        in_specs=[pl.BlockSpec((2, 128, 1536), lambda i: (0, i, 0))],
        out_specs=pl.BlockSpec((128, 1536), lambda i: (i, 0)),
        out_shape=jax.ShapeDtypeStruct((1024, 1536), BF16),
        name="sum_embed",
    )(grad_e)
    x = pl.pallas_call(
        sum_xproj,
        grid=(2, 2),
        in_specs=[pl.BlockSpec((2, 1, 1536, 128), lambda s, c: (0, c, s, 0))],
        out_specs=pl.BlockSpec((1, 1, 1536, 128), lambda s, c: (s, c, 0, 0)),
        out_shape=jax.ShapeDtypeStruct((2, 2, 1536, 128), BF16),
        name="sum_xproj",
    )(grad_x)
    c = pl.pallas_call(
        sum_chan,
        grid=(2, 2),
        in_specs=[pl.BlockSpec((2, 1, 118, 1536), lambda s, y: (0, y, 0, s))],
        out_specs=pl.BlockSpec((1, 2, 1, 4, 64, 384), lambda s, y: (s, 0, y, 0, 0, 0)),
        out_shape=jax.ShapeDtypeStruct((2, 2, 2, 4, 64, 384), BF16),
        name="sum_chan",
    )(grad_c)
    return e, x, c


def exchange(reps, inverse, *refs):
    inp = refs[0:3]
    states = refs[3:12]
    grad = refs[12:15]
    other = refs[15:18]
    norm_ref, clip_ref = refs[18:20]
    bc, b2, b3, b4 = refs[20:23], refs[23:26], refs[26:29], refs[29:32]
    piece = refs[32:35]
    held = refs[35:44]
    gpad, sq, sqr, loads, pair_s, pair_r, many_s, many_r = refs[44:52]

    rep, s = lax.axis_index("rep"), lax.axis_index("shard")
    stride_z, stride_y = reps // 4, reps // 8
    c = lax.rem(rep, 2)
    y = lax.rem(rep // stride_y, 2)
    z = rep // stride_z
    sib = (rep + 1 - 2 * c, s)
    ynb = (rep + (1 - 2 * y) * stride_y, s)
    xnb = (rep, 1 - s)
    zs = [lax.rem(z + d, 4) for d in (1, 2, 3)]
    znb = [(rep + (t - z) * stride_z, s) for t in zs]

    barrier = pltpu.get_barrier_semaphore()
    for dev in (sib, ynb, xnb, *znb):
        pl.semaphore_signal(barrier, inc=1, device_id=dev, device_id_type=MESH)
    pl.semaphore_wait(barrier, 6)

    pending = []
    count = [0, 0]

    def pair(src, dst, dev):
        k = count[0]
        count[0] += 1
        copy = pltpu.make_async_remote_copy(
            src_ref=src, dst_ref=dst, send_sem=pair_s.at[k], recv_sem=pair_r.at[k],
            device_id=dev, device_id_type=MESH)
        copy.start()
        pending.append(copy)
        return copy

    def spread(source, slot):
        k = count[1]
        count[1] += 1
        waits = []
        for d, (t, dev) in enumerate(zip(zs, znb)):
            copy = pltpu.make_async_remote_copy(
                src_ref=source(t), dst_ref=slot(z), send_sem=many_s.at[k, d],
                recv_sem=many_r.at[k, z], device_id=dev, device_id_type=MESH)
            copy.start()
            pending.append(copy)
            waits.append(pltpu.make_async_remote_copy(
                src_ref=source(t), dst_ref=slot(t), send_sem=many_s.at[k, d],
                recv_sem=many_r.at[k, t], device_id=dev, device_id_type=MESH))
        return waits

    def add(into, at_into, of, at_of, n):
        def one(k, carry):
            a, b = at_into(k), at_of(k)
            into[a] = (into[a].astype(F32) + of[b].astype(F32)).astype(BF16)
            return carry
        lax.fori_loop(0, n, one, 0)

    first = [pair(inp[i].at[:, 1 - c], bc[i], sib) for i in range(3)]

    place = y * 4 + z
    loading = []
    for k in range(3):
        row = pl.multiple_of((c * 8 + place) * 32, 32)
        loading.append(pltpu.make_async_copy(
            states[k].at[pl.ds(row, 32), :], held[k], loads.at[k]))
        row = pl.multiple_of(place * 192, 192)
        loading.append(pltpu.make_async_copy(
            states[3 + k].at[c, pl.ds(row, 192), :], held[3 + k], loads.at[3 + k]))
        col = pl.multiple_of(z * 384, 384)
        loading.append(pltpu.make_async_copy(
            states[6 + k].at[y, :, pl.ds(col, 384)], held[6 + k], loads.at[6 + k]))
    for copy in loading:
        copy.start()

    second = []
    for i in range(3):
        first[i].wait_recv()
        for half in (0, 1):
            if i == 0:
                keep = s if half else 1 - s
                add(bc[i], lambda k: (keep, k // 4, k % 4),
                    inp[i], lambda k: (keep, c, k // 4, k % 4), 8)
                if not half:
                    second.append(pair(bc[i].at[1 - s], b2[i], xnb))
            else:
                keep = y if half else 1 - y
                add(bc[i], lambda k: (k // 4, keep, k % 4),
                    inp[i], lambda k: (k // 4, c, keep, k % 4), 8)
                if not half:
                    second.append(pair(bc[i].at[:, 1 - y], b2[i], ynb))
    third = []
    for i in range(3):
        second[i].wait_recv()
        mine, dev = (y, ynb) if i == 0 else (s, xnb)
        for half in (0, 1):
            keep = mine if half else 1 - mine
            if i == 0:
                add(b2[i], lambda k: (keep, k), bc[i], lambda k: (s, keep, k), 4)
            else:
                add(b2[i], lambda k: (keep, k), bc[i], lambda k: (keep, y, k), 4)
            if not half:
                third.append(pair(b2[i].at[1 - mine], b3[i], dev))
    fourth = []
    for i in range(3):
        third[i].wait_recv()
        mine = y if i == 0 else s
        add(b3[i], lambda k: (k,), b2[i], lambda k: (mine, k), 4)
        fourth.append(spread(lambda t: b3[i].at[t], lambda t: b4[i].at[t]))

    sq[...] = jnp.zeros((8, 128), F32)
    gpad[...] = jnp.zeros((128, 384), F32)
    wave_g = []
    for i in range(3):
        for wait in fourth[i]:
            wait.wait_recv()
        rows, cols = PIECES[i]
        total = b3[i][z].astype(F32)
        for t in zs:
            total = total + b4[i][t].astype(F32)
        grad[i][c, y, z] = total.astype(BF16)
        mean = total * inverse
        tile = (mean * mean).reshape(rows // 8, 8, cols).sum(axis=0)
        part = sq[...]
        for k in range(cols // 128):
            part = part + tile[:, k * 128:k * 128 + 128]
        sq[...] = part
        wave_g.append(spread(lambda t: grad[i].at[c, y, z], lambda t: grad[i].at[c, y, t]))

    for k, dev in enumerate((sib, xnb, ynb)):
        sqr[k, 0] = sq[...]
        pair(sqr.at[k, 0], sqr.at[k, 1], dev).wait_recv()
        sq[...] = sqr[k, 0] + sqr[k, 1]
    sqr[3, z] = sq[...]
    for wait in spread(lambda t: sqr.at[3, z], lambda t: sqr.at[3, t]):
        wait.wait_recv()
    squares = jnp.sum(sqr[3, 0] + sqr[3, 1] + sqr[3, 2] + sqr[3, 3])
    norm = jnp.sqrt(jnp.full((8, 128), squares, F32))
    norm_ref[...] = norm
    clip_ref[...] = jnp.minimum(1.0, 1.0 / (norm + 1e-06))
    clip = clip_ref[0:1, 0:1]

    for copy in loading:
        copy.wait()
    row = pl.multiple_of(c * 64, 64)
    gpad[pl.ds(row, 64), :] = grad[2][c, y, z].astype(F32)
    cross = []
    for i in range(3):
        w, m, v = (held[3 * i + k][...] for k in range(3))
        if i < 2:
            g = grad[i][c, y, z].astype(F32) * inverse
            piece[i][...] = adamw_update(w, m, v, g, clip)[0].astype(BF16)
            source = piece[i]
        else:
            g = gpad[0:118, :] * inverse
            piece[i][112:128, :] = jnp.zeros((16, 384), BF16)
            piece[i][0:118, :] = adamw_update(w, m, v, g, clip)[0].astype(BF16)
            source = piece[i].at[pl.ds(row, 64), :]
        cross.append(pair(source, other[i].at[c, y, z], xnb))

    over_y = []
    for i in range(3):
        for wait in wave_g[i]:
            wait.wait_recv()
        over_y.append(pair(grad[i].at[c, y], grad[i].at[c, y], ynb))
    wave_w = []
    for i in range(3):
        cross[i].wait_recv()
        wave_w.append(spread(lambda t: other[i].at[c, y, z], lambda t: other[i].at[c, y, t]))
    over_c = []
    for i in range(3):
        over_y[i].wait_recv()
        over_c.append(pair(grad[i].at[c], grad[i].at[c], sib))
    over_y = []
    for i in range(3):
        for wait in wave_w[i]:
            wait.wait_recv()
        over_y.append(pair(other[i].at[c, y], other[i].at[c, y], ynb))
    for i in range(3):
        over_y[i].wait_recv()
        over_c.append(pair(other[i].at[c], other[i].at[c], sib))
    for copy in over_c:
        copy.wait_recv()
    for copy in pending:
        copy.wait_send()


def run_exchange(reps, inverse, sums, states):
    half = tuple(jax.ShapeDtypeStruct((2, 2, 4, *p), BF16) for p in PIECES)
    tile = jax.ShapeDtypeStruct((8, 128), F32)
    held = [pltpu.VMEM(p, F32) for p in (PIECES[0], PIECES[1], (118, 384)) for _ in range(3)]
    scratch = [pltpu.VMEM((2, 2, 4, *p), BF16) for p in PIECES]
    scratch += [pltpu.VMEM((2, 4, *p), BF16) for p in PIECES]
    scratch += [pltpu.VMEM((4, *p), BF16) for p in PIECES]
    scratch += [pltpu.VMEM((4, *p), BF16) for p in PIECES]
    scratch += [pltpu.VMEM(p, BF16) for p in (PIECES[0], PIECES[1], (128, 384))]
    scratch += held
    scratch += [
        pltpu.VMEM((128, 384), F32),
        pltpu.VMEM((8, 128), F32),
        pltpu.VMEM((4, 4, 8, 128), F32),
        pltpu.SemaphoreType.DMA((9,)),
        pltpu.SemaphoreType.DMA((27,)),
        pltpu.SemaphoreType.DMA((27,)),
        pltpu.SemaphoreType.DMA((10, 3)),
        pltpu.SemaphoreType.DMA((10, 4)),
    ]
    return pl.pallas_call(
        functools.partial(exchange, reps, inverse),
        out_shape=half + half + (tile, tile),
        in_specs=[VMEM] * 3 + [HBM] * 9,
        out_specs=[VMEM] * 8,
        scratch_shapes=scratch,
        compiler_params=pltpu.CompilerParams(
            collective_id=0, has_side_effects=True, vmem_limit_bytes=LIMIT),
        name="exchange",
    )(*sums, *states)


def finish_rows(inverse, lead, clip_ref, g_ref, o_ref, w, m, v, nw, nm, nv, full):
    s = lax.axis_index("shard")
    clip = clip_ref[0:1, 0:1]
    new = adamw_update(w[...], m[...], v[...], g_ref[...].astype(F32) * inverse, clip)
    nw[...], nm[...], nv[...] = new
    if lead:
        full[0, s] = new[0][0].astype(BF16)
        full[0, 1 - s] = o_ref[0]
    else:
        full[s] = new[0].astype(BF16)
        full[1 - s] = o_ref[...]


def finish_chan(inverse, clip_ref, g_ref, o_ref, w, m, v, nw, nm, nv, full):
    s = lax.axis_index("shard")
    clip = clip_ref[0:1, 0:1]
    for c in range(2):
        rows = 64 if c == 0 else TAIL
        for z in range(4):
            at = (0, slice(c * 64, c * 64 + rows), slice(z * 384, z * 384 + 384))
            g = g_ref[c, 0, z, 0:rows].astype(F32) * inverse
            new = adamw_update(w[at], m[at], v[at], g, clip)
            nw[at], nm[at], nv[at] = new
            own = pl.multiple_of(s * 1536 + z * 384, 128)
            far = pl.multiple_of((1 - s) * 1536 + z * 384, 128)
            full[0, c * 64:c * 64 + rows, pl.ds(own, 384)] = new[0].astype(BF16)
            full[0, c * 64:c * 64 + rows, pl.ds(far, 384)] = o_ref[c, 0, z, 0:rows]


def finish(inverse, clip, grads, others, states):
    params = pltpu.CompilerParams(vmem_limit_bytes=LIMIT)
    tile = pl.BlockSpec((8, 128), lambda *i: (0, 0))
    results = []
    block = pl.BlockSpec((128, 1536), lambda i: (i, 0))
    state = jax.ShapeDtypeStruct((512, 1536), F32)
    results.append(pl.pallas_call(
        functools.partial(finish_rows, inverse, False),
        grid=(4,),
        in_specs=[tile] + [block] * 5,
        out_specs=[block] * 3 + [pl.BlockSpec((2, 128, 1536), lambda i: (0, i, 0))],
        out_shape=[state] * 3 + [jax.ShapeDtypeStruct((2, 512, 1536), BF16)],
        compiler_params=params, name="finish_embed",
    )(clip, grads[0].reshape(512, 1536), others[0].reshape(512, 1536), *states[0:3]))
    block = pl.BlockSpec((1, 768, 128), lambda l, i: (l, i, 0))
    state = jax.ShapeDtypeStruct((2, 1536, 128), F32)
    results.append(pl.pallas_call(
        functools.partial(finish_rows, inverse, True),
        grid=(2, 2),
        in_specs=[tile] + [block] * 5,
        out_specs=[block] * 3 + [pl.BlockSpec((1, 2, 768, 128), lambda l, i: (l, 0, i, 0))],
        out_shape=[state] * 3 + [jax.ShapeDtypeStruct((2, 2, 1536, 128), BF16)],
        compiler_params=params, name="finish_xproj",
    )(clip, grads[1].reshape(2, 1536, 128), others[1].reshape(2, 1536, 128), *states[3:6]))
    block = pl.BlockSpec((1, 118, 1536), lambda l: (l, 0, 0))
    part = pl.BlockSpec((2, 1, 4, 64, 384), lambda l: (0, l, 0, 0, 0))
    state = jax.ShapeDtypeStruct((2, 118, 1536), F32)
    results.append(pl.pallas_call(
        functools.partial(finish_chan, inverse),
        grid=(2,),
        in_specs=[tile, part, part] + [block] * 3,
        out_specs=[block] * 3 + [pl.BlockSpec((1, 118, 3072), lambda l: (l, 0, 0))],
        out_shape=[state] * 3 + [jax.ShapeDtypeStruct((2, 118, 3072), BF16)],
        compiler_params=params, name="finish_chan",
    )(clip, grads[2], others[2], *states[6:9]))
    return results


def on_device(gx, gc, ge, wx, wc, we, mx, mc, me, vx, vc, ve):
    reps, shards = lax.axis_size("rep"), lax.axis_size("shard")
    inverse = 1.0 / (gx.shape[0] * reps * shards)
    sums = local_sums(ge, gx, gc)
    extra = reps // 16
    if extra > 1:
        groups = [[z * (reps // 4) + y * (reps // 8) + e * 2 + c for e in range(extra)]
                  for z in range(4) for y in range(2) for c in range(2)]
        sums = [lax.psum(v.astype(F32), "rep", axis_index_groups=groups).astype(BF16)
                for v in sums]
    sums = [v.reshape(2, 2, 2, 4, *p) for v, p in zip(sums, PIECES)]
    states = (we, me, ve, wx, mx, vx, wc, mc, vc)
    out = run_exchange(reps, inverse, sums, states)
    norm, clip = out[6], out[7]
    (nwe, nme, nve, fe), (nwx, nmx, nvx, fx), (nwc, nmc, nvc, fc) = finish(
        inverse, clip, out[0:3], out[3:6], states)
    return (nwx, nwc, nwe, nmx, nmc, nme, nvx, nvc, nve,
            fx.reshape(2, 3072, 128), fc, fe.reshape(1024, 1536), norm[0, 0:1])


def solution(mesh):
    rows, cols, lead = P(None, "shard", None), P(None, None, "shard"), P("shard", None)
    spread = ("rep", "shard")
    return jax.shard_map(
        on_device,
        mesh=mesh,
        in_specs=(P(spread, None, None, None), P(spread, None, None, None),
                  P(spread, None, None)) + (rows, cols, lead) * 3,
        out_specs=(rows, cols, lead) * 3 + (P(), P(), P(), P()),
        check_vma=False,
    )
```

```python
import functools

import jax
import jax.numpy as jnp
from jax import lax
from jax.experimental import pallas as pl
from jax.experimental.pallas import tpu as pltpu
from jax.sharding import PartitionSpec as P

beta_one = 0.9
beta_two = 0.999
learn_rate = 0.003
decay_rate = 0.1
epsilon = 1e-08
correct_one = 0.9999734386011124
correct_two = 0.09520785288629094

F32 = jnp.float32
BF16 = jnp.bfloat16
MESH = pl.DeviceIdType.MESH
VMEM = pl.BlockSpec(memory_space=pltpu.VMEM)
HBM = pl.BlockSpec(memory_space=pl.ANY)
PIECES = ((32, 768), (32, 768), (192, 128), (64, 384))
TAIL = 54
LIMIT = 52 * 1024 * 1024


def adamw_update(weight, moment, second, gradient, clip_factor):
    clipped = clip_factor * gradient
    new_moment = beta_one * moment + (1.0 - beta_one) * clipped
    new_second = beta_two * second + (1.0 - beta_two) * clipped * clipped
    root = jnp.sqrt(new_second * (1.0 / correct_two)) + epsilon
    step_size = new_moment * (1.0 / correct_one) / root
    new_weight = weight - learn_rate * (step_size + decay_rate * weight)
    return (new_weight, new_moment, new_second)


def add_pair(first, second):
    return (first.astype(F32) + second.astype(F32)).astype(BF16)


def sum_kernel(e_ref, x_ref, left, right, x_out):
    left[...] = add_pair(e_ref[0, :, 0:768], e_ref[1, :, 0:768])
    right[...] = add_pair(e_ref[0, :, 768:1536], e_ref[1, :, 768:1536])
    x_out[0] = add_pair(x_ref[0], x_ref[1])


def sum_chan(g_ref, o_ref):
    for c in range(2):
        rows = 64 if c == 0 else TAIL
        for z in range(4):
            at = (0, slice(c * 64, c * 64 + rows), slice(z * 384, z * 384 + 384))
            total = g_ref[(0, *at)].astype(F32) + g_ref[(1, *at)].astype(F32)
            if rows < 64:
                o_ref[0, c, 0, z] = jnp.zeros((64, 384), BF16)
            o_ref[0, c, 0, z, 0:rows] = total.astype(BF16)


def local_sums(grad_e, grad_x, grad_c):
    half = jax.ShapeDtypeStruct((1024, 768), BF16)
    left, right, x = pl.pallas_call(
        sum_kernel,
        grid=(8,),
        in_specs=[pl.BlockSpec((2, 128, 1536), lambda i: (0, i, 0)),
                  pl.BlockSpec((2, 2, 384, 128), lambda i: (0, 0, i, 0))],
        out_specs=[pl.BlockSpec((128, 768), lambda i: (i, 0)),
                   pl.BlockSpec((128, 768), lambda i: (i, 0)),
                   pl.BlockSpec((1, 2, 384, 128), lambda i: (i // 4, 0, i % 4, 0))],
        out_shape=[half, half, jax.ShapeDtypeStruct((2, 2, 1536, 128), BF16)],
        name="local_sum",
    )(grad_e, grad_x)
    c = pl.pallas_call(
        sum_chan,
        grid=(2, 2),
        in_specs=[pl.BlockSpec((2, 1, 118, 1536), lambda s, y: (0, y, 0, s))],
        out_specs=pl.BlockSpec((1, 2, 1, 4, 64, 384), lambda s, y: (s, 0, y, 0, 0, 0)),
        out_shape=jax.ShapeDtypeStruct((2, 2, 2, 4, 64, 384), BF16),
        name="sum_chan",
    )(grad_c)
    return left, right, x, c


def exchange(reps, inverse, *refs):
    inp = refs[0:4]
    states = refs[4:13]
    grad = refs[13:17]
    other = refs[17:21]
    norm_ref, clip_ref = refs[21:23]
    bc, b2, b3, b4 = refs[23:27], refs[27:31], refs[31:35], refs[35:39]
    piece = refs[39:43]
    held = refs[43:55]
    gpad, sq, sqr, loads, pair_s, pair_r, many_s, many_r = refs[55:63]

    rep, s = lax.axis_index("rep"), lax.axis_index("shard")
    stride_z, stride_y = reps // 4, reps // 8
    c = lax.rem(rep, 2)
    y = lax.rem(rep // stride_y, 2)
    z = rep // stride_z
    sib = (rep + 1 - 2 * c, s)
    ynb = (rep + (1 - 2 * y) * stride_y, s)
    xnb = (rep, 1 - s)
    zs = [lax.rem(z + d, 4) for d in (1, 2, 3)]
    znb = [(rep + (t - z) * stride_z, s) for t in zs]

    barrier = pltpu.get_barrier_semaphore()
    for dev in (sib, ynb, xnb, *znb):
        pl.semaphore_signal(barrier, inc=1, device_id=dev, device_id_type=MESH)
    pl.semaphore_wait(barrier, 6)

    pending = []
    count = [0, 0]

    def pair(src, dst, dev):
        k = count[0]
        count[0] += 1
        copy = pltpu.make_async_remote_copy(
            src_ref=src, dst_ref=dst, send_sem=pair_s.at[k], recv_sem=pair_r.at[k],
            device_id=dev, device_id_type=MESH)
        copy.start()
        pending.append(copy)
        return copy

    def spread(source, slot):
        k = count[1]
        count[1] += 1
        waits = []
        for d, (t, dev) in enumerate(zip(zs, znb)):
            copy = pltpu.make_async_remote_copy(
                src_ref=source(t), dst_ref=slot(z), send_sem=many_s.at[k, d],
                recv_sem=many_r.at[k, z], device_id=dev, device_id_type=MESH)
            copy.start()
            pending.append(copy)
            waits.append(pltpu.make_async_remote_copy(
                src_ref=source(t), dst_ref=slot(t), send_sem=many_s.at[k, d],
                recv_sem=many_r.at[k, t], device_id=dev, device_id_type=MESH))
        return waits

    def add(into, at_into, of, at_of, n):
        def one(k, carry):
            a, b = at_into(k), at_of(k)
            into[a] = (into[a].astype(F32) + of[b].astype(F32)).astype(BF16)
            return carry
        lax.fori_loop(0, n, one, 0)

    first = [pair(inp[i].at[:, 1 - c], bc[i], sib) for i in range(4)]

    loading = []
    for k in range(3):
        row = pl.multiple_of(c * 256, 256)
        for h in range(2):
            loading.append(pltpu.make_async_copy(
                states[k].at[pl.ds(row, 256), pl.ds(h * 768, 768)],
                held[3 * h + k], loads.at[3 * h + k]))
        row = pl.multiple_of(y * 768, 768)
        loading.append(pltpu.make_async_copy(
            states[3 + k].at[c, pl.ds(row, 768), :], held[6 + k], loads.at[6 + k]))
        loading.append(pltpu.make_async_copy(states[6 + k].at[y], held[9 + k], loads.at[9 + k]))
    for copy in loading:
        copy.start()

    second = []
    for i in range(4):
        first[i].wait_recv()
        for half in (0, 1):
            if i < 2:
                keep = s if half else 1 - s
                add(bc[i], lambda k: (keep, k // 4, k % 4),
                    inp[i], lambda k: (keep, c, k // 4, k % 4), 8)
                if not half:
                    second.append(pair(bc[i].at[1 - s], b2[i], xnb))
            else:
                keep = y if half else 1 - y
                add(bc[i], lambda k: (k // 4, keep, k % 4),
                    inp[i], lambda k: (k // 4, c, keep, k % 4), 8)
                if not half:
                    second.append(pair(bc[i].at[:, 1 - y], b2[i], ynb))
    third = []
    for i in range(4):
        second[i].wait_recv()
        mine, dev = (y, ynb) if i < 2 else (s, xnb)
        for half in (0, 1):
            keep = mine if half else 1 - mine
            if i < 2:
                add(b2[i], lambda k: (keep, k), bc[i], lambda k: (s, keep, k), 4)
            else:
                add(b2[i], lambda k: (keep, k), bc[i], lambda k: (keep, y, k), 4)
            if not half:
                third.append(pair(b2[i].at[1 - mine], b3[i], dev))
    fourth = []
    for i in range(4):
        third[i].wait_recv()
        mine = y if i < 2 else s
        add(b3[i], lambda k: (k,), b2[i], lambda k: (mine, k), 4)
        fourth.append(spread(lambda t: b3[i].at[t], lambda t: b4[i].at[t]))

    sq[...] = jnp.zeros((8, 128), F32)
    gpad[...] = jnp.zeros((128, 384), F32)
    piece[3][:, 112:128, :] = jnp.zeros((4, 16, 384), BF16)
    wave_g = []
    for i in range(4):
        for wait in fourth[i]:
            wait.wait_recv()
        rows, cols = PIECES[i]
        total = b3[i][z].astype(F32)
        for t in zs:
            total = total + b4[i][t].astype(F32)
        grad[i][c, y, z] = total.astype(BF16)
        mean = total * inverse
        tile = (mean * mean).reshape(rows // 8, 8, cols).sum(axis=0)
        part = sq[...]
        for k in range(cols // 128):
            part = part + tile[:, k * 128:k * 128 + 128]
        sq[...] = part
        wave_g.append(spread(lambda t: grad[i].at[c, y, z], lambda t: grad[i].at[c, y, t]))

    for k, dev in enumerate((sib, xnb, ynb)):
        sqr[k, 0] = sq[...]
        pair(sqr.at[k, 0], sqr.at[k, 1], dev).wait_recv()
        sq[...] = sqr[k, 0] + sqr[k, 1]
    sqr[3, z] = sq[...]
    for wait in spread(lambda t: sqr.at[3, z], lambda t: sqr.at[3, t]):
        wait.wait_recv()
    squares = jnp.sum(sqr[3, 0] + sqr[3, 1] + sqr[3, 2] + sqr[3, 3])
    norm = jnp.sqrt(jnp.full((8, 128), squares, F32))
    norm_ref[...] = norm
    clip_ref[...] = jnp.minimum(1.0, 1.0 / (norm + 1e-06))
    clip = clip_ref[0:1, 0:1]

    for copy in loading:
        copy.wait()

    def update(i, at_y):
        rows = PIECES[i][0]

        def one(k, carry):
            first_row = (at_y * 4 + k) * rows if i < 2 else k * rows
            at = pl.ds(pl.multiple_of(first_row, rows), rows)
            w, m, v = (held[3 * i + q][at, :] for q in range(3))
            g = grad[i][c, at_y, k].astype(F32) * inverse
            new = adamw_update(w, m, v, g, clip)[0].astype(BF16)
            if i < 2:
                piece[i][at_y, k] = new
            else:
                piece[i][k] = new
            return carry

        def one_chan(k, carry):
            row, col = pl.multiple_of(c * 64, 64), pl.multiple_of(k * 384, 384)
            w, m, v = (held[9 + q][:, pl.ds(col, 384)] for q in range(3))
            gpad[pl.ds(row, 64), :] = grad[3][c, at_y, k].astype(F32) * inverse
            new = adamw_update(w, m, v, gpad[0:118, :], clip)[0]
            piece[3][k, 0:118, :] = new.astype(BF16)
            return carry

        lax.fori_loop(0, 4, one_chan if i == 3 else one, 0)
        if i == 3:
            source = piece[3].at[:, pl.ds(pl.multiple_of(c * 64, 64), 64), :]
            return pair(source, other[3].at[c, at_y], xnb)
        source = piece[i].at[at_y] if i < 2 else piece[i]
        return pair(source, other[i].at[c, at_y], xnb)

    over_y, cross, over_c = [], [], []
    for i in range(4):
        for wait in wave_g[i]:
            wait.wait_recv()
        over_y.append(pair(grad[i].at[c, y], grad[i].at[c, y], ynb))
        cross.append(update(i, y))
    cross_far = []
    for i in range(4):
        over_y[i].wait_recv()
        over_c.append(pair(grad[i].at[c], grad[i].at[c], sib))
        if i < 2:
            cross_far.append(update(i, 1 - y))
    over_y = []
    for i in (2, 3):
        cross[i].wait_recv()
        over_y.append(pair(other[i].at[c, y], other[i].at[c, y], ynb))
    for i in (0, 1):
        cross[i].wait_recv()
        cross_far[i].wait_recv()
        over_c.append(pair(other[i].at[c], other[i].at[c], sib))
    for i in (2, 3):
        over_y[i - 2].wait_recv()
        over_c.append(pair(other[i].at[c], other[i].at[c], sib))
    for copy in over_c:
        copy.wait_recv()
    for copy in pending:
        copy.wait_send()


def run_exchange(reps, inverse, sums, states):
    half = tuple(jax.ShapeDtypeStruct((2, 2, 4, *p), BF16) for p in PIECES)
    tile = jax.ShapeDtypeStruct((8, 128), F32)
    held = [pltpu.VMEM(p, F32) for p in ((256, 768), (256, 768), (768, 128), (118, 1536))
            for _ in range(3)]
    scratch = [pltpu.VMEM((2, 2, 4, *p), BF16) for p in PIECES]
    scratch += [pltpu.VMEM((2, 4, *p), BF16) for p in PIECES]
    scratch += [pltpu.VMEM((4, *p), BF16) for p in PIECES]
    scratch += [pltpu.VMEM((4, *p), BF16) for p in PIECES]
    scratch += [pltpu.VMEM(n, BF16) for n in (
        (2, 4, 32, 768), (2, 4, 32, 768), (4, 192, 128), (4, 128, 384))]
    scratch += held
    scratch += [
        pltpu.VMEM((128, 384), F32),
        pltpu.VMEM((8, 128), F32),
        pltpu.VMEM((4, 4, 8, 128), F32),
        pltpu.SemaphoreType.DMA((12,)),
        pltpu.SemaphoreType.DMA((40,)),
        pltpu.SemaphoreType.DMA((40,)),
        pltpu.SemaphoreType.DMA((10, 3)),
        pltpu.SemaphoreType.DMA((10, 4)),
    ]
    return pl.pallas_call(
        functools.partial(exchange, reps, inverse),
        out_shape=half + half + (tile, tile),
        in_specs=[VMEM] * 4 + [HBM] * 9,
        out_specs=[VMEM] * 10,
        scratch_shapes=scratch,
        compiler_params=pltpu.CompilerParams(
            collective_id=0, has_side_effects=True, vmem_limit_bytes=LIMIT),
        name="exchange",
    )(*sums, *states)


def finish_kernel(inverse, clip_ref, *refs):
    g, o, st = refs[0:4], refs[4:8], refs[8:17]
    out, full_e, full_x, full_c = refs[17:26], refs[26], refs[27], refs[28]
    s = lax.axis_index("shard")
    clip = clip_ref[0:1, 0:1]

    def step(k, at, grad):
        w, m, v = (st[k + q][at] for q in range(3))
        new = adamw_update(w, m, v, grad.astype(F32) * inverse, clip)
        for q in range(3):
            out[k + q][at] = new[q]
        return new[0].astype(BF16)

    for h in range(2):
        at = (slice(None), slice(h * 768, h * 768 + 768))
        full_e[(s, *at)] = step(0, at, g[h][...])
        full_e[(1 - s, *at)] = o[h][...]
    for layer in range(2):
        full_x[layer, s] = step(3, (layer,), g[2][layer])
        full_x[layer, 1 - s] = o[2][layer]
    for c in range(2):
        rows = 64 if c == 0 else TAIL
        at = (0, slice(c * 64, c * 64 + rows), slice(None))
        full_c[(s, *at)] = step(6, at, g[3][c, 0, 0, 0:rows])
        full_c[(1 - s, *at)] = o[3][c, 0, 0, 0:rows]


def finish(inverse, clip, grads, others, states):
    tile = pl.BlockSpec((8, 128), lambda i: (0, 0))
    half = pl.BlockSpec((64, 768), lambda i: (i, 0))
    e = pl.BlockSpec((64, 1536), lambda i: (i, 0))
    x = pl.BlockSpec((2, 192, 128), lambda i: (0, i, 0))
    c = pl.BlockSpec((1, 118, 384), lambda i: (i // 4, 0, i % 4))
    part = pl.BlockSpec((2, 1, 1, 64, 384), lambda i: (0, i // 4, i % 4, 0, 0))
    views = ((512, 768), (512, 768), (2, 1536, 128), (2, 2, 4, 64, 384))
    g = [v.reshape(n) for v, n in zip(grads, views)]
    o = [v.reshape(n) for v, n in zip(others, views)]
    shapes = ((512, 1536), (2, 1536, 128), (2, 118, 1536))
    out = pl.pallas_call(
        functools.partial(finish_kernel, inverse),
        grid=(8,),
        in_specs=[tile, half, half, x, part, half, half, x, part] + [e] * 3 + [x] * 3 + [c] * 3,
        out_specs=[e] * 3 + [x] * 3 + [c] * 3 + [
            pl.BlockSpec((2, 64, 1536), lambda i: (0, i, 0)),
            pl.BlockSpec((2, 2, 192, 128), lambda i: (0, 0, i, 0)),
            pl.BlockSpec((2, 1, 118, 384), lambda i: (0, i // 4, 0, i % 4))],
        out_shape=[jax.ShapeDtypeStruct(n, F32) for n in shapes for _ in range(3)] + [
            jax.ShapeDtypeStruct((2, 512, 1536), BF16),
            jax.ShapeDtypeStruct((2, 2, 1536, 128), BF16),
            jax.ShapeDtypeStruct((2, 2, 118, 1536), BF16)],
        compiler_params=pltpu.CompilerParams(vmem_limit_bytes=LIMIT),
        name="finish",
    )(clip, *g, *o, *states)
    full_c = out[11].transpose(1, 2, 0, 3).reshape(2, 118, 3072)
    return out, full_c


def on_device(gx, gc, ge, wx, wc, we, mx, mc, me, vx, vc, ve):
    reps, shards = lax.axis_size("rep"), lax.axis_size("shard")
    inverse = 1.0 / (gx.shape[0] * reps * shards)
    sums = local_sums(ge, gx, gc)
    extra = reps // 16
    if extra > 1:
        groups = [[z * (reps // 4) + y * (reps // 8) + e * 2 + c for e in range(extra)]
                  for z in range(4) for y in range(2) for c in range(2)]
        sums = [lax.psum(v.astype(F32), "rep", axis_index_groups=groups).astype(BF16)
                for v in sums]
    sums = [v.reshape(2, 2, 2, 4, *p) for v, p in zip(sums, PIECES)]
    states = (we, me, ve, wx, mx, vx, wc, mc, vc)
    out = run_exchange(reps, inverse, sums, states)
    norm, clip = out[8], out[9]
    new, full_c = finish(inverse, clip, out[0:4], out[4:8], states)
    nwe, nme, nve, nwx, nmx, nvx = new[0:6]
    nwc, nmc, nvc = new[6:9]
    return (nwx, nwc, nwe, nmx, nmc, nme, nvx, nvc, nve,
            new[10].reshape(2, 3072, 128), full_c, new[9].reshape(1024, 1536), norm[0, 0:1])


def solution(mesh):
    rows, cols, lead = P(None, "shard", None), P(None, None, "shard"), P("shard", None)
    spread = ("rep", "shard")
    return jax.shard_map(
        on_device,
        mesh=mesh,
        in_specs=(P(spread, None, None, None), P(spread, None, None, None),
                  P(spread, None, None)) + (rows, cols, lead) * 3,
        out_specs=(rows, cols, lead) * 3 + (P(), P(), P(), P()),
        check_vma=False,
    )
```
